32 devices in a mesh: groups: 2 (over y), expert: 8 (over z, x), tensor: 2 (over core).
Axes of the slice: x: 2, y: 2, z: 4, core: 2. Of those that a mesh axis runs over, the one named last changes fastest.
Arguments:
- tokens: bfloat16 [2, 1024, 2048], P(None, ('groups', 'expert')), parts along dimension 1, may hold values from -6 to 6
- routes: int32 [2, 1024, 8], P(None, ('groups', 'expert')), parts along dimension 1, may hold values from 0 to 7, as said below
- probs: float32 [2, 1024, 8], P(None, ('groups', 'expert')), parts along dimension 1, may hold values from 0.02 to 0.3
- up_weight: bfloat16 [8, 2048, 768], P('expert', None, 'tensor'), may hold values from -0.125 to 0.125
- down_weight: bfloat16 [8, 768, 2048], P('expert', None, 'tensor'), may hold values from -0.21875 to 0.21875
- old_place: int32 [16], P('groups'), parts along dimension 0, may hold values from 0 to 7, as said below
- new_place: int32 [32], P('groups'), parts along dimension 0, may hold values from 0 to 7, as said below
Outputs:
- mixed: bfloat16 [2, 1024, 2048], P(None, ('groups', 'expert'), 'tensor'), parts along dimension 1
- slot_rows: int32 [32], P(('groups', 'expert')), parts along dimension 0
The draws below stay inside these ranges and needn't reach their ends.
There are 2 independent parts, one for each index of `groups`. The reference program is written for one: setup_inputs(seed, part) draws one part's arguments, and reference() takes and returns one part's arrays. A program takes and returns all parts, laid end to end along the dimension named above; an argument that names none is the same for every part. Nothing has to cross between parts.
Inputs may be any that keep to these rules, and one draw needn't show every extreme that they name: `routes`: each token names 8 different experts. `old_place`: each expert is held by exactly one old slot. `new_place`: new slot 2 * s holds the expert of old slot s; no expert is held by more than 4 new slots, and some expert by exactly 4.
All inputs are finite; a program needn't handle non-finite values.
Results may differ from the reference program's by a relative error of at most 0.0058.
Values may be sent and summed in bfloat16 or wider, within the bound.
A program may use at most 128 MiB of HBM per device.

```python
import math
import jax
import jax.numpy as jnp
from jax import lax

D = 2048
FF = 768
TOPK = 8
MB = 2
REPLICAS = 4
TOK_DEV = 64
EXPERTS = 8
SLOTS = 16
TOKENS = 512
CAPACITY = 64
SLOT_CAP = 40
N_EXPERT = 8


def popularity(key):
    return jax.random.permutation(jax.random.fold_in(key, 7001), EXPERTS).astype(jnp.int32)


def draw_old_place(key, part):
    return jax.random.permutation(jax.random.fold_in(key, 7002), EXPERTS).astype(jnp.int32)


def draw_new_place(key, part):
    old_place = draw_old_place(key, part)
    order = popularity(key)
    eighth = EXPERTS // 8
    spots = jnp.arange(EXPERTS, dtype=jnp.int32)
    middle = eighth + (spots - 3 * eighth) // 2
    tail = 2 * eighth + (spots - 5 * eighth)
    rank_pick = jnp.where(spots < 3 * eighth, spots // 3, jnp.where(spots < 5 * eighth, middle, tail))
    extras = order[rank_pick]
    extras = jax.random.permutation(jax.random.fold_in(key, 7003), extras)
    return jnp.stack([old_place, extras], axis=1).reshape(-1).astype(jnp.int32)


def draw_routes(key, part):
    order = popularity(key)
    rank_of = jnp.zeros((EXPERTS,), jnp.int32).at[order].set(jnp.arange(EXPERTS, dtype=jnp.int32))
    eighth = EXPERTS // 8
    bias = jnp.where(rank_of < eighth, 14418, jnp.where(rank_of < 2 * eighth, 3932, 0)).astype(jnp.int32)
    noise = jax.random.randint(jax.random.fold_in(key, 7004), (MB, TOKENS, EXPERTS), 0, 65536, dtype=jnp.int32)
    labels = jnp.arange(EXPERTS, dtype=jnp.int32)
    scores = (noise + bias[None, None, :]) * EXPERTS + labels[None, None, :]
    picked = lax.top_k(scores, TOPK)[1]
    return picked.astype(jnp.int32)


def shard_levels(key, extent, cuts, least, largest):
    factor_of, own = 1.0, jax.random.fold_in(key, 6)
    for position, parts in cuts:
        steps = jnp.exp(jax.random.uniform(jax.random.fold_in(own, position), (parts,), jnp.float32, least / len(cuts), largest / len(cuts)))
        factor_of = factor_of * jnp.repeat(steps, extent[position] // parts).reshape([-1 if axis == position else 1 for axis in range(len(extent))])
    return factor_of


def normal_values(rng, dims, deviation, reach, split=(), held_as=jnp.bfloat16):
    values = deviation * jax.random.normal(rng, dims, jnp.float32)
    if split:
        values = values * shard_levels(rng, dims, split, -0.22, 0.18)
    return jnp.clip(values, -reach, reach).astype(held_as)


def setup_inputs(seed: int = 0, part: int = 0) -> dict:
    key_list = jax.random.split(jax.random.key(seed), 8)
    part_keys = jax.random.split(jax.random.fold_in(key_list[7], part), 8)
    tokens = normal_values(part_keys[0], (MB, TOKENS, D), 1.0, 6.0, ((1, 8),))
    routes = draw_routes(jax.random.fold_in(jax.random.fold_in(key_list[7], part), 71), part)
    probs = jnp.clip(jnp.exp(math.log(0.3) - 2.7080503 * jax.random.uniform(part_keys[2], (MB, TOKENS, TOPK), jnp.float32) ** shard_levels(part_keys[2], (MB, TOKENS, TOPK), ((1, 8),), -0.2, 0.2)), 0.02, 0.3)
    up_weight = normal_values(key_list[3], (EXPERTS, D, FF), D ** -0.5, 0.125, ((0, 8), (2, 2)))
    down_weight = normal_values(key_list[4], (EXPERTS, FF, D), FF ** -0.5, 0.21875, ((0, 8), (2, 2)))
    old_place = draw_old_place(jax.random.fold_in(jax.random.fold_in(key_list[7], part), 71), part)
    new_place = draw_new_place(jax.random.fold_in(jax.random.fold_in(key_list[7], part), 71), part)
    return dict(tokens=tokens, routes=routes, probs=probs, up_weight=up_weight, down_weight=down_weight, old_place=old_place, new_place=new_place)


def block_ranks(labels):
    positions = jnp.arange(labels.shape[1]).astype(jnp.int32)
    earlier = positions[None, :] < positions[:, None]

    def one_block(row):
        same_label = row[:, None] == row[None, :]
        return jnp.sum((same_label & earlier).astype(jnp.int32), axis=1).astype(jnp.int32)

    return lax.map(one_block, labels)


def expert_rows(tokens_mb, probs_mb, routes_mb, kept, up_weight, down_weight, old_place, bound):
    flat_routes = routes_mb.reshape(-1)
    flat_kept = kept.reshape(-1)
    flat_probs = probs_mb.reshape(-1)
    row_total = flat_routes.shape[0]

    def one_slot(total, slot_items):
        up_mat, down_mat, expert_id = slot_items
        wanted = (flat_routes == expert_id) & flat_kept
        chosen = jnp.nonzero(wanted, size=bound, fill_value=row_total)[0].astype(jnp.int32)
        safe = jnp.minimum(chosen, row_total - 1)
        token_ids = safe // TOPK
        hidden = jax.nn.silu(jnp.dot(tokens_mb[token_ids], up_mat, preferred_element_type=jnp.float32)).astype(jnp.bfloat16)
        rounded = jnp.dot(hidden, down_mat, preferred_element_type=jnp.float32).astype(jnp.bfloat16)
        outputs = lax.optimization_barrier(rounded).astype(jnp.float32)
        scales = jnp.where(chosen < row_total, flat_probs[safe], jnp.zeros_like(flat_probs[safe]))
        return total.at[token_ids].add(outputs * scales[:, None]), None

    start = jnp.zeros((tokens_mb.shape[0], D), jnp.float32)
    total, unused = lax.scan(one_slot, start, (up_weight, down_weight, old_place))
    return total.astype(jnp.bfloat16)


def reference(tokens, routes, probs, up_weight, down_weight, old_place, new_place):
    slot_ids = jnp.arange(EXPERTS).astype(jnp.int32)
    home = jnp.zeros((EXPERTS,), jnp.int32).at[old_place].set(slot_ids)
    early_blocks = routes[0].reshape(N_EXPERT, TOK_DEV * TOPK)
    early_kept = block_ranks(home[early_blocks]) < CAPACITY
    later_blocks = routes[1].reshape(N_EXPERT, TOK_DEV * TOPK)
    new_ids = jnp.arange(SLOTS).astype(jnp.int32)
    same_slot = new_place[:, None] == new_place[None, :]
    occurrence = jnp.sum((same_slot & (new_ids[None, :] < new_ids[:, None])).astype(jnp.int32), axis=1).astype(jnp.int32)
    replicas = jnp.zeros((EXPERTS,), jnp.int32).at[new_place].add(jnp.ones((SLOTS,), jnp.int32))
    table = jnp.zeros((EXPERTS, REPLICAS), jnp.int32).at[new_place, occurrence].set(new_ids)
    sources = jnp.arange(N_EXPERT).astype(jnp.int32)[:, None]
    wanted = (block_ranks(later_blocks) + sources) % replicas[later_blocks]
    later_slots = table[later_blocks, wanted]
    later_kept = block_ranks(later_slots) < SLOT_CAP
    early_out = expert_rows(tokens[0], probs[0], routes[0], early_kept, up_weight, down_weight, old_place, N_EXPERT * CAPACITY)
    later_bound = N_EXPERT * min(REPLICAS * SLOT_CAP, TOK_DEV)
    later_out = expert_rows(tokens[1], probs[1], routes[1], later_kept, up_weight, down_weight, old_place, later_bound)
    slot_rows = jnp.zeros((SLOTS,), jnp.int32).at[later_slots.reshape(-1)].add(jnp.ones((N_EXPERT * TOK_DEV * TOPK,), jnp.int32))
    return jnp.stack([early_out, later_out]), slot_rows
```

```python
import functools

import jax
import jax.numpy as jnp
from jax import lax
from jax.experimental import pallas as pl
from jax.experimental.pallas import tpu as pltpu
from jax.sharding import PartitionSpec as P

MESH = pl.DeviceIdType.MESH

REPLICAS = 4


def earlier_same(labels):
    positions = jnp.arange(labels.shape[0], dtype=jnp.int32)
    earlier = positions[None, :] < positions[:, None]
    same_label = labels[:, None] == labels[None, :]
    return jnp.sum((earlier & same_label).astype(jnp.int32), axis=1)


def holder_index(labels, holders):
    matches = labels[:, None] == holders[None, :]
    positions = jnp.arange(holders.shape[0], dtype=jnp.int32)
    return jnp.sum(matches.astype(jnp.int32) * positions[None, :], axis=1)


def replica_slots(flat_routes, new_place, source_index):
    positions = jnp.arange(new_place.shape[0], dtype=jnp.int32)
    same_slot = new_place[:, None] == new_place[None, :]
    occurrence = jnp.sum(
        (same_slot & (positions[None, :] < positions[:, None])).astype(jnp.int32), axis=1
    )
    matches = flat_routes[:, None] == new_place[None, :]
    replicas = jnp.sum(matches.astype(jnp.int32), axis=1)
    wanted = (earlier_same(flat_routes) + source_index) % replicas
    chosen = matches & (occurrence[None, :] == wanted[:, None])
    slot_ids = jnp.sum(chosen.astype(jnp.int32) * positions[None, :], axis=1)
    return (slot_ids, chosen)


def capacity_for(block_rows, targets, token_count):
    return min(token_count, max(2, (5 * block_rows + 4 * targets - 1) // (4 * targets)))


def serve_cells(tokens_mb, probs_mb, cell_ids, target_count, block, up_local, down_local):
    token_count = tokens_mb.shape[0]
    topk_count = cell_ids.shape[0] // token_count
    slots_here = up_local.shape[0]
    cells = jnp.arange(target_count * block, dtype=jnp.int32)
    placed = (cells[:, None] == cell_ids[None, :]).astype(jnp.bfloat16)
    by_token = jnp.sum(placed.reshape(target_count * block, token_count, topk_count), axis=2)
    send_rows = jnp.dot(by_token, tokens_mb, preferred_element_type=jnp.float32).astype(
        jnp.bfloat16
    )
    send_rows = send_rows.reshape(target_count, block, -1)
    received = lax.all_to_all(send_rows, "expert", split_axis=0, concat_axis=0, tiled=True)
    sources = received.shape[0] // slots_here
    grid = received.reshape(sources, slots_here, received.shape[1], received.shape[2])
    hidden = jax.nn.silu(
        jnp.einsum("nscd,sdf->nscf", grid, up_local, preferred_element_type=jnp.float32)
    ).astype(jnp.bfloat16)
    hidden = lax.all_gather(hidden, "tensor", axis=3, tiled=True)
    outputs = jnp.einsum(
        "nscf,sfd->nscd", hidden, down_local, preferred_element_type=jnp.float32
    ).astype(jnp.bfloat16)
    outputs = outputs.reshape(received.shape[0], received.shape[1], -1)
    returned = lax.all_to_all(outputs, "expert", split_axis=0, concat_axis=0, tiled=True)
    flat_back = returned.reshape(target_count * block, -1)
    picked = lax.dot_general(
        placed, flat_back, (((0,), (0,)), ((), ())), preferred_element_type=jnp.float32
    )
    weighted = picked.reshape(token_count, topk_count, -1) * probs_mb[:, :, None]
    return jnp.sum(weighted, axis=1).astype(jnp.bfloat16)


def on_device(tokens, routes, probs, up_weight, down_weight, old_place, new_place):
    source_index = lax.axis_index("expert")
    devices = lax.axis_size("expert")
    token_count = tokens.shape[1]
    topk_count = routes.shape[2]
    block_rows = token_count * topk_count
    expert_count = old_place.shape[0]
    slot_count = new_place.shape[0]
    early_cap = capacity_for(block_rows, expert_count, token_count)
    later_cap = capacity_for(block_rows, slot_count, token_count)
    early_routes = routes[0].reshape(-1)
    later_routes = routes[1].reshape(-1)
    early_slots = holder_index(early_routes, old_place)
    early_rank = earlier_same(early_slots)
    early_cells = jnp.where(early_rank < early_cap, early_slots * early_cap + early_rank, -1)
    later_slots, chosen = replica_slots(later_routes, new_place, source_index)
    slot_counts = lax.psum(jnp.sum(chosen.astype(jnp.int32), axis=0), "expert")
    slot_dev = slot_count // devices
    slot_rows = lax.dynamic_slice_in_dim(slot_counts, source_index * slot_dev, slot_dev, 0)
    later_rank = earlier_same(later_slots)
    later_kept = later_rank < later_cap
    early_out = serve_cells(
        tokens[0], probs[0], early_cells, expert_count, early_cap, up_weight, down_weight
    )
    homes = holder_index(later_routes, old_place)
    home_block = min(token_count, REPLICAS * later_cap)
    home_labels = jnp.where(later_kept, homes, -1)
    home_rank = earlier_same(home_labels)
    later_cells = jnp.where(later_kept, homes * home_block + home_rank, -1)
    later_out = serve_cells(
        tokens[1], probs[1], later_cells, expert_count, home_block, up_weight, down_weight
    )
    return (jnp.stack([early_out, later_out]), slot_rows)


def dense_weights(routes, probs, old_place, new_place):
    token_count = routes.shape[1]
    block_rows = token_count * routes.shape[2]
    early_cap = capacity_for(block_rows, old_place.shape[0], token_count)
    later_cap = capacity_for(block_rows, new_place.shape[0], token_count)
    replicas = jnp.sum((old_place[:, None] == new_place[None, :]).astype(jnp.int32), axis=1)
    rank = jnp.arange(token_count, dtype=jnp.int32)[None, :]
    early_kept = jnp.broadcast_to(rank < early_cap, (old_place.shape[0], token_count))
    later_kept = rank < later_cap * replicas[:, None]
    kept = jnp.stack([early_kept, later_kept])
    same = routes[:, None, :, :] == old_place[None, :, None, None]
    weights = jnp.sum(jnp.where(same, probs[:, None, :, :], 0.0), axis=3)
    return jnp.where(kept, weights, 0.0)


def dense_slot_rows(new_place, source_index, devices, token_count):
    slot_count = new_place.shape[0]
    slot_dev = slot_count // devices
    positions = jnp.arange(slot_count, dtype=jnp.int32)
    same = new_place[:, None] == new_place[None, :]
    replicas = jnp.sum(same.astype(jnp.int32), axis=1)
    earlier = positions[None, :] < positions[:, None]
    occurrence = jnp.sum((same & earlier).astype(jnp.int32), axis=1)
    places = jnp.arange(token_count, dtype=jnp.int32)[:, None] + jnp.arange(devices, dtype=jnp.int32)[None, :]
    hits = (places[None] % replicas[:, None, None]) == occurrence[:, None, None]
    counts = jnp.sum(hits.astype(jnp.int32), axis=(1, 2))
    return lax.dynamic_slice_in_dim(counts, source_index * slot_dev, slot_dev, 0)


def expert_kernel(
    n, chunks, tok, wts, up, down, out,
    xall, wall, upv, downv, acc, psend, xrecv, zsend, zrecv, res,
    loc, tw_s, tw_r, w_s, w_r, az_s, az_r, ax_s, ax_r, rx_s, rx_r, rz_s, rz_r,
):
    e = lax.axis_index("expert")
    core = lax.axis_index("tensor")
    column = n // 2
    x = lax.rem(e, 2)
    z = e // 2
    pair = e + 1 - 2 * x
    rows, width = xall.shape[1], xall.shape[2]
    step_rows = rows // chunks
    up_half = up.shape[2]
    halves = downv.shape[0]
    half = downv.shape[2]

    def remote(src, dst, send, recv, expert=None):
        device = {"expert": expert} if expert is not None else {"tensor": 1 - core}
        return pltpu.make_async_remote_copy(
            src_ref=src, dst_ref=dst, send_sem=send, recv_sem=recv,
            device_id=device, device_id_type=MESH,
        )

    def column_id(step):
        return lax.rem(z - step + column, column)

    def block(step, side):
        return 2 * column_id(step) + side

    local = [
        pltpu.make_async_copy(tok.at[core], xall.at[e], loc.at[0]),
        pltpu.make_async_copy(wts.at[core], wall.at[e], loc.at[1]),
        pltpu.make_async_copy(
            up.at[0], upv.at[:, pl.ds(pl.multiple_of(core * up_half, 128), up_half)], loc.at[2]
        ),
        pltpu.make_async_copy(down.at[0], downv.at[core], loc.at[3]),
    ]
    for copy in local:
        copy.start()

    barrier = pltpu.get_barrier_semaphore()
    for shift in range(1, n):
        pl.semaphore_signal(barrier, inc=1, device_id={"expert": lax.rem(e + shift, n)}, device_id_type=MESH)
    pl.semaphore_signal(barrier, inc=1, device_id={"tensor": 1 - core}, device_id_type=MESH)
    pl.semaphore_wait(barrier, n)

    def part(k):
        return pl.ds(k * step_rows, step_rows)

    own_x, own_z, own_w = [], [], []
    for k in range(chunks):
        copy = remote(tok.at[core, part(k)], xall.at[e, part(k)], ax_s.at[0, k], ax_r.at[0, k], pair)
        copy.start()
        own_x.append(copy)
    for s in range(1, column):
        for k in range(chunks):
            target = 2 * lax.rem(z + s, column) + x
            copy = remote(tok.at[core, part(k)], xall.at[e, part(k)], az_s.at[s, k], az_r.at[s, k], target)
            copy.start()
            own_z.append(copy)
    swap = [
        remote(
            up.at[0], upv.at[:, pl.ds(pl.multiple_of(core * up_half, 128), up_half)], tw_s.at[0], tw_r.at[0]
        ),
        remote(down.at[0], downv.at[core], tw_s.at[1], tw_r.at[1]),
    ]
    for copy in swap:
        copy.start()
    for s in range(1, n):
        copy = remote(wts.at[core], wall.at[e], w_s.at[s], w_r.at[s], lax.rem(e + s, n))
        copy.start()
        own_w.append(copy)

    sent = []

    def relay(s):
        b = block(s, x)
        for k in range(chunks):
            remote(tok.at[core, part(k)], xall.at[b, part(k)], az_s.at[s, k], az_r.at[s, k], pair).wait_recv()
            copy = remote(xall.at[b, part(k)], xall.at[b, part(k)], ax_s.at[s, k], ax_r.at[s, k], pair)
            copy.start()
            sent.append(copy)

    def arrived(s):
        b = block(s, 1 - x)
        for k in range(chunks):
            remote(tok.at[core, part(k)], xall.at[b, part(k)], ax_s.at[s, k], ax_r.at[s, k], pair).wait_recv()

    def scale_of(b):
        row = wall[b, pl.ds(e, 1), :]
        square = lax.broadcasted_iota(jnp.int32, (rows, rows), 0) == lax.broadcasted_iota(jnp.int32, (rows, rows), 1)
        return jnp.sum(jnp.where(square, row, 0.0), axis=1, keepdims=True)

    def hidden_of(b):
        v = jnp.dot(xall[b], upv[...], preferred_element_type=jnp.float32)
        return (v / (1.0 + jnp.exp(-v))).astype(jnp.bfloat16)

    def keep(s):
        b = block(s, x)
        h = hidden_of(b)
        scale = scale_of(b)
        for q in range(halves):
            acc[s, q] = jnp.dot(h, downv[q], preferred_element_type=jnp.float32) * scale

    def give(s):
        b = block(s, 1 - x)
        h = hidden_of(b)
        scale = scale_of(b)
        for q in range(halves):
            o = jnp.dot(h, downv[q], preferred_element_type=jnp.float32) * scale
            psend[s, q] = o.astype(jnp.bfloat16)
            copy = remote(psend.at[s, q], xrecv.at[s, q], rx_s.at[s, q], rx_r.at[s, q], pair)
            copy.start()
            sent.append(copy)

    def pass_on(s):
        for q in range(halves):
            remote(psend.at[s, q], xrecv.at[s, q], rx_s.at[s, q], rx_r.at[s, q], pair).wait_recv()
            zsend[s, q] = (acc[s, q] + xrecv[s, q].astype(jnp.float32)).astype(jnp.bfloat16)
            copy = remote(zsend.at[s, q], zrecv.at[s, q], rz_s.at[s, q], rz_r.at[s, q], block(s, x))
            copy.start()
            sent.append(copy)

    for copy in local:
        copy.wait()
    for copy in swap:
        copy.wait_recv()
    for s in range(1, n):
        remote(wts.at[core], wall.at[lax.rem(e - s + n, n)], w_s.at[s], w_r.at[s], pair).wait_recv()
    keep(0)
    relay(1)
    arrived(0)
    give(0)
    for s in range(1, column):
        if s + 1 < column:
            relay(s + 1)
        keep(s)
        arrived(s)
        give(s)
        if s > 1:
            pass_on(s - 1)
    if column > 1:
        pass_on(column - 1)
    for q in range(halves):
        remote(psend.at[0, q], xrecv.at[0, q], rx_s.at[0, q], rx_r.at[0, q], pair).wait_recv()
        total = acc[0, q] + xrecv[0, q].astype(jnp.float32)
        for s in range(1, column):
            remote(zsend.at[s, q], zrecv.at[s, q], rz_s.at[s, q], rz_r.at[s, q], pair).wait_recv()
            total = total + zrecv[s, q].astype(jnp.float32)
        res[q] = total.astype(jnp.bfloat16)
    last = remote(res.at[1 - core], out.at[core], tw_s.at[2], tw_r.at[2])
    last.start()
    mine = pltpu.make_async_copy(res.at[core], out.at[core], loc.at[4])
    mine.start()
    for copy in own_x + own_z + own_w + swap + sent:
        copy.wait_send()
    mine.wait()
    last.wait_send()
    remote(res.at[1 - core], out.at[1 - core], tw_s.at[2], tw_r.at[2]).wait_recv()


def dense_on_device(tokens, routes, probs, up_weight, down_weight, old_place, new_place):
    source_index = lax.axis_index("expert")
    n = lax.axis_size("expert")
    batches, rows, width = tokens.shape
    hidden_half, half = down_weight.shape[1] // 2, down_weight.shape[2]
    column, chunks = n // 2, 2
    slot_rows = dense_slot_rows(new_place, source_index, n, rows)
    weights = dense_weights(routes, probs, old_place, new_place)
    dma = pltpu.SemaphoreType.DMA
    bf16, f32 = jnp.bfloat16, jnp.float32
    mixed = pl.pallas_call(
        functools.partial(expert_kernel, n, chunks),
        out_shape=jax.ShapeDtypeStruct((batches, rows, half), bf16),
        in_specs=[pl.BlockSpec(memory_space=pl.ANY)] * 4,
        out_specs=pl.BlockSpec(memory_space=pl.ANY),
        scratch_shapes=[
            pltpu.VMEM((n, rows, width), bf16),
            pltpu.VMEM((n, old_place.shape[0], rows), f32),
            pltpu.VMEM((width, 2 * hidden_half), bf16),
            pltpu.VMEM((2, 2 * hidden_half, half), bf16),
            pltpu.VMEM((column, 2, rows, half), f32),
            pltpu.VMEM((column, 2, rows, half), bf16),
            pltpu.VMEM((column, 2, rows, half), bf16),
            pltpu.VMEM((column, 2, rows, half), bf16),
            pltpu.VMEM((column, 2, rows, half), bf16),
            pltpu.VMEM((2, rows, half), bf16),
            dma((5,)), dma((3,)), dma((3,)), dma((n,)), dma((n,)),
            dma((column, chunks)), dma((column, chunks)), dma((column, chunks)), dma((column, chunks)),
            dma((column, 2)), dma((column, 2)), dma((column, 2)), dma((column, 2)),
        ],
        compiler_params=pltpu.CompilerParams(
            collective_id=0, has_side_effects=True, vmem_limit_bytes=40 * 1024 * 1024
        ),
    )(tokens, weights, up_weight, down_weight)
    return (mixed, slot_rows)


def choose_plan(tokens, routes, probs, up_weight, down_weight, old_place, new_place):
    n = lax.axis_size("expert")
    rows = tokens.shape[1]
    dense = (
        routes.shape[2] == old_place.shape[0] == n
        and n % 2 == 0
        and lax.axis_size("tensor") == tokens.shape[0] == 2
        and up_weight.shape[0] == 1
        and rows % 32 == 0
        and up_weight.shape[2] % 128 == 0
    )
    plan = dense_on_device if dense else on_device
    return plan(tokens, routes, probs, up_weight, down_weight, old_place, new_place)


def solution(mesh):
    placed = (
        P(None, ("groups", "expert"), None),
        P(None, ("groups", "expert"), None),
        P(None, ("groups", "expert"), None),
        P("expert", None, "tensor"),
        P("expert", None, "tensor"),
        P("groups"),
        P("groups"),
    )
    return jax.shard_map(
        choose_plan,
        mesh=mesh,
        in_specs=placed,
        out_specs=(P(None, ("groups", "expert"), "tensor"), P(("groups", "expert"))),
        check_vma=False,
    )
```

```python
import functools

import jax
import jax.numpy as jnp
from jax import lax
from jax.experimental import pallas as pl
from jax.experimental.pallas import tpu as pltpu
from jax.sharding import PartitionSpec as P

MESH = pl.DeviceIdType.MESH

REPLICAS = 4


def earlier_same(labels):
    positions = jnp.arange(labels.shape[0], dtype=jnp.int32)
    earlier = positions[None, :] < positions[:, None]
    same_label = labels[:, None] == labels[None, :]
    return jnp.sum((earlier & same_label).astype(jnp.int32), axis=1)


def holder_index(labels, holders):
    matches = labels[:, None] == holders[None, :]
    positions = jnp.arange(holders.shape[0], dtype=jnp.int32)
    return jnp.sum(matches.astype(jnp.int32) * positions[None, :], axis=1)


def replica_slots(flat_routes, new_place, source_index):
    positions = jnp.arange(new_place.shape[0], dtype=jnp.int32)
    same_slot = new_place[:, None] == new_place[None, :]
    occurrence = jnp.sum(
        (same_slot & (positions[None, :] < positions[:, None])).astype(jnp.int32), axis=1
    )
    matches = flat_routes[:, None] == new_place[None, :]
    replicas = jnp.sum(matches.astype(jnp.int32), axis=1)
    wanted = (earlier_same(flat_routes) + source_index) % replicas
    chosen = matches & (occurrence[None, :] == wanted[:, None])
    slot_ids = jnp.sum(chosen.astype(jnp.int32) * positions[None, :], axis=1)
    return (slot_ids, chosen)


def capacity_for(block_rows, targets, token_count):
    return min(token_count, max(2, (5 * block_rows + 4 * targets - 1) // (4 * targets)))


def serve_cells(tokens_mb, probs_mb, cell_ids, target_count, block, up_local, down_local):
    token_count = tokens_mb.shape[0]
    topk_count = cell_ids.shape[0] // token_count
    slots_here = up_local.shape[0]
    cells = jnp.arange(target_count * block, dtype=jnp.int32)
    placed = (cells[:, None] == cell_ids[None, :]).astype(jnp.bfloat16)
    by_token = jnp.sum(placed.reshape(target_count * block, token_count, topk_count), axis=2)
    send_rows = jnp.dot(by_token, tokens_mb, preferred_element_type=jnp.float32).astype(
        jnp.bfloat16
    )
    send_rows = send_rows.reshape(target_count, block, -1)
    received = lax.all_to_all(send_rows, "expert", split_axis=0, concat_axis=0, tiled=True)
    sources = received.shape[0] // slots_here
    grid = received.reshape(sources, slots_here, received.shape[1], received.shape[2])
    hidden = jax.nn.silu(
        jnp.einsum("nscd,sdf->nscf", grid, up_local, preferred_element_type=jnp.float32)
    ).astype(jnp.bfloat16)
    hidden = lax.all_gather(hidden, "tensor", axis=3, tiled=True)
    outputs = jnp.einsum(
        "nscf,sfd->nscd", hidden, down_local, preferred_element_type=jnp.float32
    ).astype(jnp.bfloat16)
    outputs = outputs.reshape(received.shape[0], received.shape[1], -1)
    returned = lax.all_to_all(outputs, "expert", split_axis=0, concat_axis=0, tiled=True)
    flat_back = returned.reshape(target_count * block, -1)
    picked = lax.dot_general(
        placed, flat_back, (((0,), (0,)), ((), ())), preferred_element_type=jnp.float32
    )
    weighted = picked.reshape(token_count, topk_count, -1) * probs_mb[:, :, None]
    return jnp.sum(weighted, axis=1).astype(jnp.bfloat16)


def on_device(tokens, routes, probs, up_weight, down_weight, old_place, new_place):
    source_index = lax.axis_index("expert")
    devices = lax.axis_size("expert")
    token_count = tokens.shape[1]
    topk_count = routes.shape[2]
    block_rows = token_count * topk_count
    expert_count = old_place.shape[0]
    slot_count = new_place.shape[0]
    early_cap = capacity_for(block_rows, expert_count, token_count)
    later_cap = capacity_for(block_rows, slot_count, token_count)
    early_routes = routes[0].reshape(-1)
    later_routes = routes[1].reshape(-1)
    early_slots = holder_index(early_routes, old_place)
    early_rank = earlier_same(early_slots)
    early_cells = jnp.where(early_rank < early_cap, early_slots * early_cap + early_rank, -1)
    later_slots, chosen = replica_slots(later_routes, new_place, source_index)
    slot_counts = lax.psum(jnp.sum(chosen.astype(jnp.int32), axis=0), "expert")
    slot_dev = slot_count // devices
    slot_rows = lax.dynamic_slice_in_dim(slot_counts, source_index * slot_dev, slot_dev, 0)
    later_rank = earlier_same(later_slots)
    later_kept = later_rank < later_cap
    early_out = serve_cells(
        tokens[0], probs[0], early_cells, expert_count, early_cap, up_weight, down_weight
    )
    homes = holder_index(later_routes, old_place)
    home_block = min(token_count, REPLICAS * later_cap)
    home_labels = jnp.where(later_kept, homes, -1)
    home_rank = earlier_same(home_labels)
    later_cells = jnp.where(later_kept, homes * home_block + home_rank, -1)
    later_out = serve_cells(
        tokens[1], probs[1], later_cells, expert_count, home_block, up_weight, down_weight
    )
    return (jnp.stack([early_out, later_out]), slot_rows)


def dense_weights(routes, probs, old_place, new_place):
    token_count = routes.shape[1]
    block_rows = token_count * routes.shape[2]
    early_cap = capacity_for(block_rows, old_place.shape[0], token_count)
    later_cap = capacity_for(block_rows, new_place.shape[0], token_count)
    replicas = jnp.sum((old_place[:, None] == new_place[None, :]).astype(jnp.int32), axis=1)
    rank = jnp.arange(token_count, dtype=jnp.int32)[None, :]
    early_kept = jnp.broadcast_to(rank < early_cap, (old_place.shape[0], token_count))
    later_kept = rank < later_cap * replicas[:, None]
    kept = jnp.stack([early_kept, later_kept])
    same = routes[:, None, :, :] == old_place[None, :, None, None]
    weights = jnp.sum(jnp.where(same, probs[:, None, :, :], 0.0), axis=3)
    return jnp.where(kept, weights, 0.0)


def dense_slot_rows(new_place, source_index, devices, token_count):
    slot_count = new_place.shape[0]
    slot_dev = slot_count // devices
    positions = jnp.arange(slot_count, dtype=jnp.int32)
    same = new_place[:, None] == new_place[None, :]
    replicas = jnp.sum(same.astype(jnp.int32), axis=1)
    earlier = positions[None, :] < positions[:, None]
    occurrence = jnp.sum((same & earlier).astype(jnp.int32), axis=1)
    places = jnp.arange(token_count, dtype=jnp.int32)[:, None] + jnp.arange(devices, dtype=jnp.int32)[None, :]
    hits = (places[None] % replicas[:, None, None]) == occurrence[:, None, None]
    counts = jnp.sum(hits.astype(jnp.int32), axis=(1, 2))
    return lax.dynamic_slice_in_dim(counts, source_index * slot_dev, slot_dev, 0)


def expert_kernel(
    n, chunks, tok, wts, up, down, out,
    xall, wall, upv, downv, acc, psend, xrecv, zsend, zrecv, res,
    loc, tw_s, tw_r, w_s, w_r, own_s, az_s, az_r, ax_s, ax_r, rx_s, rx_r, rz_s, rz_r,
):
    e = lax.axis_index("expert")
    core = lax.axis_index("tensor")
    column = n // 2
    x = lax.rem(e, 2)
    z = e // 2
    pair = e + 1 - 2 * x
    rows, width = xall.shape[1], xall.shape[2]
    step_rows = rows // chunks
    up_half = up.shape[2]
    halves = downv.shape[0]
    half = downv.shape[2]

    def remote(src, dst, send, recv, expert=None):
        device = {"expert": expert} if expert is not None else {"tensor": 1 - core}
        return pltpu.make_async_remote_copy(
            src_ref=src, dst_ref=dst, send_sem=send, recv_sem=recv,
            device_id=device, device_id_type=MESH,
        )

    def place(p):
        if p == 0:
            return z, 0, 0
        near = jnp.minimum(z, column - 1 - z)
        both = p <= 2 * near
        distance = jnp.where(both, (p + 1) // 2, p - near)
        away = jnp.where(both, 1 - 2 * (p % 2), jnp.where(z > near, 1, -1))
        return z - away * distance, distance, away

    def block(p, side):
        return 2 * place(p)[0] + side

    local = [
        pltpu.make_async_copy(tok.at[core], xall.at[e], loc.at[0]),
        pltpu.make_async_copy(wts.at[core], wall.at[e], loc.at[1]),
        pltpu.make_async_copy(
            up.at[0], upv.at[:, pl.ds(pl.multiple_of(core * up_half, 128), up_half)], loc.at[2]
        ),
        pltpu.make_async_copy(down.at[0], downv.at[core], loc.at[3]),
    ]
    for copy in local:
        copy.start()

    barrier = pltpu.get_barrier_semaphore()
    for shift in range(1, n):
        pl.semaphore_signal(barrier, inc=1, device_id={"expert": lax.rem(e + shift, n)}, device_id_type=MESH)
    pl.semaphore_signal(barrier, inc=1, device_id={"tensor": 1 - core}, device_id_type=MESH)
    pl.semaphore_wait(barrier, n)

    def part(k):
        return pl.ds(k * step_rows, step_rows)

    def inside(position):
        return (position >= 0) & (position < column)

    own_x, own_w, sent, guarded = [], [], [], []

    def send_if(condition, copy):
        pl.when(condition)(copy.start)
        guarded.append((condition, copy))

    for k in range(chunks):
        copy = remote(tok.at[core, part(k)], xall.at[e, part(k)], ax_s.at[0, k], ax_r.at[0, k], pair)
        copy.start()
        own_x.append(copy)
        for side in range(2):
            target = z + 1 - 2 * side
            send_if(inside(target), remote(
                tok.at[core, part(k)], xall.at[e, part(k)], own_s.at[side, k], az_r.at[z, k], 2 * target + x
            ))
    swap = [
        remote(
            up.at[0], upv.at[:, pl.ds(pl.multiple_of(core * up_half, 128), up_half)], tw_s.at[0], tw_r.at[0]
        ),
        remote(down.at[0], downv.at[core], tw_s.at[1], tw_r.at[1]),
    ]
    for copy in swap:
        copy.start()
    for s in range(1, n):
        copy = remote(wts.at[core], wall.at[e], w_s.at[s], w_r.at[s], lax.rem(e + s, n))
        copy.start()
        own_w.append(copy)

    def relay(p):
        j, distance, away = place(p)
        b = 2 * j + x
        for k in range(chunks):
            remote(tok.at[core, part(k)], xall.at[b, part(k)], az_s.at[p, k], az_r.at[j, k], pair).wait_recv()
            send_if(inside(z + away), remote(
                xall.at[b, part(k)], xall.at[b, part(k)], az_s.at[p, k], az_r.at[j, k], 2 * (z + away) + x
            ))
            copy = remote(xall.at[b, part(k)], xall.at[b, part(k)], ax_s.at[p, k], ax_r.at[p, k], pair)
            copy.start()
            sent.append(copy)

    def arrived(s):
        b = block(s, 1 - x)
        for k in range(chunks):
            remote(tok.at[core, part(k)], xall.at[b, part(k)], ax_s.at[s, k], ax_r.at[s, k], pair).wait_recv()

    def scale_of(b):
        row = wall[b, pl.ds(e, 1), :]
        square = lax.broadcasted_iota(jnp.int32, (rows, rows), 0) == lax.broadcasted_iota(jnp.int32, (rows, rows), 1)
        return jnp.sum(jnp.where(square, row, 0.0), axis=1, keepdims=True)

    def hidden_of(b):
        v = jnp.dot(xall[b], upv[...], preferred_element_type=jnp.float32)
        return (v / (1.0 + jnp.exp(-v))).astype(jnp.bfloat16)

    def keep(s):
        b = block(s, x)
        h = hidden_of(b)
        scale = scale_of(b)
        for q in range(halves):
            acc[s, q] = jnp.dot(h, downv[q], preferred_element_type=jnp.float32) * scale

    def offer(s):
        b = block(s, 1 - x)
        h = hidden_of(b)
        scale = scale_of(b)
        for q in range(halves):
            o = jnp.dot(h, downv[q], preferred_element_type=jnp.float32) * scale
            psend[s, q] = o.astype(jnp.bfloat16)
            if s == column - 1:
                give(s, q)

    def give(s, q):
        copy = remote(psend.at[s, q], xrecv.at[s, q], rx_s.at[s, q], rx_r.at[s, q], pair)
        copy.start()
        sent.append(copy)

    def pass_on(p):
        j, distance, away = place(p)
        slot = jnp.where((distance == 1) & (away < 0), column, j)
        outer = inside(z + away)
        for q in range(halves):
            remote(psend.at[p, q], xrecv.at[p, q], rx_s.at[p, q], rx_r.at[p, q], pair).wait_recv()

            @pl.when(outer)
            def _():
                remote(zsend.at[p, q], zrecv.at[j, q], rz_s.at[p, q], rz_r.at[j, q], pair).wait_recv()
                total = acc[p, q] + xrecv[p, q].astype(jnp.float32) + zrecv[j, q].astype(jnp.float32)
                zsend[p, q] = total.astype(jnp.bfloat16)

            @pl.when(jnp.logical_not(outer))
            def _():
                zsend[p, q] = (acc[p, q] + xrecv[p, q].astype(jnp.float32)).astype(jnp.bfloat16)

            copy = remote(zsend.at[p, q], zrecv.at[slot, q], rz_s.at[p, q], rz_r.at[slot, q], 2 * (z - away) + x)
            copy.start()
            sent.append(copy)

    if column > 1:
        relay(1)
    for copy in local:
        copy.wait()
    for copy in swap:
        copy.wait_recv()
    for s in range(1, n):
        remote(wts.at[core], wall.at[lax.rem(e - s + n, n)], w_s.at[s], w_r.at[s], pair).wait_recv()
    keep(0)
    for p in range(2, column):
        relay(p)
        keep(p - 1)
    for p in range(column):
        if p == column - 1 and p > 0:
            keep(p)
        arrived(p)
        offer(p)
    for p in range(column - 2, -1, -1):
        for q in range(halves):
            give(p, q)
    for p in range(column - 1, 0, -1):
        pass_on(p)
    for q in range(halves):
        remote(psend.at[0, q], xrecv.at[0, q], rx_s.at[0, q], rx_r.at[0, q], pair).wait_recv()
        acc[0, q] += xrecv[0, q].astype(jnp.float32)
        for side, slot in ((1, z), (-1, column)):

            @pl.when(inside(z + side))
            def _():
                remote(zsend.at[0, q], zrecv.at[slot, q], rz_s.at[0, q], rz_r.at[slot, q], pair).wait_recv()
                acc[0, q] += zrecv[slot, q].astype(jnp.float32)

        res[q] = acc[0, q].astype(jnp.bfloat16)
    last = remote(res.at[1 - core], out.at[core], tw_s.at[2], tw_r.at[2])
    last.start()
    mine = pltpu.make_async_copy(res.at[core], out.at[core], loc.at[4])
    mine.start()
    for copy in own_x + own_w + swap + sent:
        copy.wait_send()
    for condition, copy in guarded:
        pl.when(condition)(copy.wait_send)
    mine.wait()
    last.wait_send()
    remote(res.at[1 - core], out.at[1 - core], tw_s.at[2], tw_r.at[2]).wait_recv()


def dense_on_device(tokens, routes, probs, up_weight, down_weight, old_place, new_place):
    source_index = lax.axis_index("expert")
    n = lax.axis_size("expert")
    batches, rows, width = tokens.shape
    hidden_half, half = down_weight.shape[1] // 2, down_weight.shape[2]
    column, chunks = n // 2, 2
    slot_rows = dense_slot_rows(new_place, source_index, n, rows)
    weights = dense_weights(routes, probs, old_place, new_place)
    dma = pltpu.SemaphoreType.DMA
    bf16, f32 = jnp.bfloat16, jnp.float32
    mixed = pl.pallas_call(
        functools.partial(expert_kernel, n, chunks),
        out_shape=jax.ShapeDtypeStruct((batches, rows, half), bf16),
        in_specs=[pl.BlockSpec(memory_space=pl.ANY)] * 4,
        out_specs=pl.BlockSpec(memory_space=pl.ANY),
        scratch_shapes=[
            pltpu.VMEM((n, rows, width), bf16),
            pltpu.VMEM((n, old_place.shape[0], rows), f32),
            pltpu.VMEM((width, 2 * hidden_half), bf16),
            pltpu.VMEM((2, 2 * hidden_half, half), bf16),
            pltpu.VMEM((column, 2, rows, half), f32),
            pltpu.VMEM((column, 2, rows, half), bf16),
            pltpu.VMEM((column, 2, rows, half), bf16),
            pltpu.VMEM((column, 2, rows, half), bf16),
            pltpu.VMEM((column + 1, 2, rows, half), bf16),
            pltpu.VMEM((2, rows, half), bf16),
            dma((5,)), dma((3,)), dma((3,)), dma((n,)), dma((n,)),
            dma((2, chunks)), dma((column, chunks)), dma((column, chunks)), dma((column, chunks)), dma((column, chunks)),
            dma((column, 2)), dma((column, 2)), dma((column, 2)), dma((column + 1, 2)),
        ],
        compiler_params=pltpu.CompilerParams(
            collective_id=0, has_side_effects=True, vmem_limit_bytes=60 * 1024 * 1024
        ),
    )(tokens, weights, up_weight, down_weight)
    return (mixed, slot_rows)


def choose_plan(tokens, routes, probs, up_weight, down_weight, old_place, new_place):
    n = lax.axis_size("expert")
    rows = tokens.shape[1]
    dense = (
        routes.shape[2] == old_place.shape[0] == n
        and n % 2 == 0
        and lax.axis_size("tensor") == tokens.shape[0] == 2
        and up_weight.shape[0] == 1
        and rows % 32 == 0
        and up_weight.shape[2] % 128 == 0
    )
    plan = dense_on_device if dense else on_device
    return plan(tokens, routes, probs, up_weight, down_weight, old_place, new_place)


def solution(mesh):
    placed = (
        P(None, ("groups", "expert"), None),
        P(None, ("groups", "expert"), None),
        P(None, ("groups", "expert"), None),
        P("expert", None, "tensor"),
        P("expert", None, "tensor"),
        P("groups"),
        P("groups"),
    )
    return jax.shard_map(
        choose_plan,
        mesh=mesh,
        in_specs=placed,
        out_specs=(P(None, ("groups", "expert"), "tensor"), P(("groups", "expert"))),
        check_vma=False,
    )
```

```python
import functools

import jax
import jax.numpy as jnp
from jax import lax
from jax.experimental import pallas as pl
from jax.experimental.pallas import tpu as pltpu
from jax.sharding import PartitionSpec as P

MESH = pl.DeviceIdType.MESH

REPLICAS = 4


def earlier_same(labels):
    positions = jnp.arange(labels.shape[0], dtype=jnp.int32)
    earlier = positions[None, :] < positions[:, None]
    same_label = labels[:, None] == labels[None, :]
    return jnp.sum((earlier & same_label).astype(jnp.int32), axis=1)


def holder_index(labels, holders):
    matches = labels[:, None] == holders[None, :]
    positions = jnp.arange(holders.shape[0], dtype=jnp.int32)
    return jnp.sum(matches.astype(jnp.int32) * positions[None, :], axis=1)


def replica_slots(flat_routes, new_place, source_index):
    positions = jnp.arange(new_place.shape[0], dtype=jnp.int32)
    same_slot = new_place[:, None] == new_place[None, :]
    occurrence = jnp.sum(
        (same_slot & (positions[None, :] < positions[:, None])).astype(jnp.int32), axis=1
    )
    matches = flat_routes[:, None] == new_place[None, :]
    replicas = jnp.sum(matches.astype(jnp.int32), axis=1)
    wanted = (earlier_same(flat_routes) + source_index) % replicas
    chosen = matches & (occurrence[None, :] == wanted[:, None])
    slot_ids = jnp.sum(chosen.astype(jnp.int32) * positions[None, :], axis=1)
    return (slot_ids, chosen)


def capacity_for(block_rows, targets, token_count):
    return min(token_count, max(2, (5 * block_rows + 4 * targets - 1) // (4 * targets)))


def serve_cells(tokens_mb, probs_mb, cell_ids, target_count, block, up_local, down_local):
    token_count = tokens_mb.shape[0]
    topk_count = cell_ids.shape[0] // token_count
    slots_here = up_local.shape[0]
    cells = jnp.arange(target_count * block, dtype=jnp.int32)
    placed = (cells[:, None] == cell_ids[None, :]).astype(jnp.bfloat16)
    by_token = jnp.sum(placed.reshape(target_count * block, token_count, topk_count), axis=2)
    send_rows = jnp.dot(by_token, tokens_mb, preferred_element_type=jnp.float32).astype(
        jnp.bfloat16
    )
    send_rows = send_rows.reshape(target_count, block, -1)
    received = lax.all_to_all(send_rows, "expert", split_axis=0, concat_axis=0, tiled=True)
    sources = received.shape[0] // slots_here
    grid = received.reshape(sources, slots_here, received.shape[1], received.shape[2])
    hidden = jax.nn.silu(
        jnp.einsum("nscd,sdf->nscf", grid, up_local, preferred_element_type=jnp.float32)
    ).astype(jnp.bfloat16)
    hidden = lax.all_gather(hidden, "tensor", axis=3, tiled=True)
    outputs = jnp.einsum(
        "nscf,sfd->nscd", hidden, down_local, preferred_element_type=jnp.float32
    ).astype(jnp.bfloat16)
    outputs = outputs.reshape(received.shape[0], received.shape[1], -1)
    returned = lax.all_to_all(outputs, "expert", split_axis=0, concat_axis=0, tiled=True)
    flat_back = returned.reshape(target_count * block, -1)
    picked = lax.dot_general(
        placed, flat_back, (((0,), (0,)), ((), ())), preferred_element_type=jnp.float32
    )
    weighted = picked.reshape(token_count, topk_count, -1) * probs_mb[:, :, None]
    return jnp.sum(weighted, axis=1).astype(jnp.bfloat16)


def on_device(tokens, routes, probs, up_weight, down_weight, old_place, new_place):
    source_index = lax.axis_index("expert")
    devices = lax.axis_size("expert")
    token_count = tokens.shape[1]
    topk_count = routes.shape[2]
    block_rows = token_count * topk_count
    expert_count = old_place.shape[0]
    slot_count = new_place.shape[0]
    early_cap = capacity_for(block_rows, expert_count, token_count)
    later_cap = capacity_for(block_rows, slot_count, token_count)
    early_routes = routes[0].reshape(-1)
    later_routes = routes[1].reshape(-1)
    early_slots = holder_index(early_routes, old_place)
    early_rank = earlier_same(early_slots)
    early_cells = jnp.where(early_rank < early_cap, early_slots * early_cap + early_rank, -1)
    later_slots, chosen = replica_slots(later_routes, new_place, source_index)
    slot_counts = lax.psum(jnp.sum(chosen.astype(jnp.int32), axis=0), "expert")
    slot_dev = slot_count // devices
    slot_rows = lax.dynamic_slice_in_dim(slot_counts, source_index * slot_dev, slot_dev, 0)
    later_rank = earlier_same(later_slots)
    later_kept = later_rank < later_cap
    early_out = serve_cells(
        tokens[0], probs[0], early_cells, expert_count, early_cap, up_weight, down_weight
    )
    homes = holder_index(later_routes, old_place)
    home_block = min(token_count, REPLICAS * later_cap)
    home_labels = jnp.where(later_kept, homes, -1)
    home_rank = earlier_same(home_labels)
    later_cells = jnp.where(later_kept, homes * home_block + home_rank, -1)
    later_out = serve_cells(
        tokens[1], probs[1], later_cells, expert_count, home_block, up_weight, down_weight
    )
    return (jnp.stack([early_out, later_out]), slot_rows)


def dense_weights(routes, probs, old_place, new_place):
    token_count = routes.shape[1]
    block_rows = token_count * routes.shape[2]
    early_cap = capacity_for(block_rows, old_place.shape[0], token_count)
    later_cap = capacity_for(block_rows, new_place.shape[0], token_count)
    same_slot = old_place[:, None] == new_place[None, :]
    replicas = jnp.sum(same_slot.astype(jnp.int32), axis=1, keepdims=True)
    limit = jnp.where(jnp.arange(2, dtype=jnp.int32)[:, None, None] == 0, early_cap, later_cap * replicas[None])
    kept = jnp.arange(token_count, dtype=jnp.int32)[None, None, :] < limit
    same = routes[:, None, :, :] == old_place[None, :, None, None]
    return jnp.sum(jnp.where(same & kept[..., None], probs[:, None, :, :], 0.0), axis=3)


def dense_slot_rows(new_place, source_index, devices, token_count):
    slot_dev = new_place.shape[0] // devices
    mine = source_index * slot_dev + jnp.arange(slot_dev, dtype=jnp.int32)
    positions = jnp.arange(new_place.shape[0], dtype=jnp.int32)
    at_mine = mine[:, None] == positions[None, :]
    held = jnp.sum(jnp.where(at_mine, new_place[None, :], 0), axis=1)
    same = held[:, None] == new_place[None, :]
    replicas = jnp.sum(same.astype(jnp.int32), axis=1)[:, None]
    occurrence = jnp.sum((same & (positions[None, :] < mine[:, None])).astype(jnp.int32), axis=1)[:, None]
    first = jnp.arange(devices, dtype=jnp.int32)[None, :] - occurrence + replicas - 1
    counts = (first + token_count) // replicas - first // replicas
    return jnp.sum(counts, axis=1)


def expert_kernel(
    n, chunks, tok, wts, up, down, out,
    xall, wall, upv, downv, acc, psend, xrecv, zsend, zrecv, res,
    loc, tw_s, tw_r, w_s, w_r, own_s, az_s, az_r, ax_s, ax_r, rx_s, rx_r, rz_s, rz_r,
):
    e = lax.axis_index("expert")
    core = lax.axis_index("tensor")
    column = n // 2
    x = lax.rem(e, 2)
    z = e // 2
    pair = e + 1 - 2 * x
    rows, width = xall.shape[1], xall.shape[2]
    step_rows = rows // chunks
    up_half = up.shape[2]
    halves = downv.shape[0]
    half = downv.shape[2]

    def remote(src, dst, send, recv, expert=None):
        device = {"expert": expert} if expert is not None else {"tensor": 1 - core}
        return pltpu.make_async_remote_copy(
            src_ref=src, dst_ref=dst, send_sem=send, recv_sem=recv,
            device_id=device, device_id_type=MESH,
        )

    def place(p):
        if p == 0:
            return z, 0, 0
        near = jnp.minimum(z, column - 1 - z)
        both = p <= 2 * near
        distance = jnp.where(both, (p + 1) // 2, p - near)
        away = jnp.where(both, 1 - 2 * (p % 2), jnp.where(z > near, 1, -1))
        return z - away * distance, distance, away

    def block(p, side):
        return 2 * place(p)[0] + side

    local = [
        pltpu.make_async_copy(tok.at[core], xall.at[e], loc.at[0]),
        pltpu.make_async_copy(wts.at[core], wall.at[e], loc.at[1]),
        pltpu.make_async_copy(
            up.at[0], upv.at[:, pl.ds(pl.multiple_of(core * up_half, 128), up_half)], loc.at[2]
        ),
        pltpu.make_async_copy(down.at[0], downv.at[core], loc.at[3]),
    ]
    for copy in local:
        copy.start()

    barrier = pltpu.get_barrier_semaphore()
    for shift in range(1, n):
        pl.semaphore_signal(barrier, inc=1, device_id={"expert": lax.rem(e + shift, n)}, device_id_type=MESH)
    pl.semaphore_signal(barrier, inc=1, device_id={"tensor": 1 - core}, device_id_type=MESH)
    pl.semaphore_wait(barrier, n)

    def part(k):
        return pl.ds(k * step_rows, step_rows)

    def inside(position):
        return (position >= 0) & (position < column)

    own_x, own_w, sent, guarded = [], [], [], []

    def send_if(condition, copy):
        pl.when(condition)(copy.start)
        guarded.append((condition, copy))

    for k in range(chunks):
        copy = remote(tok.at[core, part(k)], xall.at[e, part(k)], ax_s.at[0, k], ax_r.at[0, k], pair)
        copy.start()
        own_x.append(copy)
        for side in range(2):
            target = z + 1 - 2 * side
            send_if(inside(target), remote(
                tok.at[core, part(k)], xall.at[e, part(k)], own_s.at[side, k], az_r.at[z, k], 2 * target + x
            ))
    swap = [
        remote(
            up.at[0], upv.at[:, pl.ds(pl.multiple_of(core * up_half, 128), up_half)], tw_s.at[0], tw_r.at[0]
        ),
        remote(down.at[0], downv.at[core], tw_s.at[1], tw_r.at[1]),
    ]
    for copy in swap:
        copy.start()
    for s in range(1, n):
        copy = remote(wts.at[core], wall.at[e], w_s.at[s], w_r.at[s], lax.rem(e + s, n))
        copy.start()
        own_w.append(copy)

    def relay(p):
        j, distance, away = place(p)
        b = 2 * j + x
        for k in range(chunks):
            remote(tok.at[core, part(k)], xall.at[b, part(k)], az_s.at[p, k], az_r.at[j, k], pair).wait_recv()
            send_if(inside(z + away), remote(
                xall.at[b, part(k)], xall.at[b, part(k)], az_s.at[p, k], az_r.at[j, k], 2 * (z + away) + x
            ))
            copy = remote(xall.at[b, part(k)], xall.at[b, part(k)], ax_s.at[p, k], ax_r.at[p, k], pair)
            copy.start()
            sent.append(copy)

    def arrived(s):
        b = block(s, 1 - x)
        for k in range(chunks):
            remote(tok.at[core, part(k)], xall.at[b, part(k)], ax_s.at[s, k], ax_r.at[s, k], pair).wait_recv()

    def scale_of(b):
        row = wall[b, pl.ds(e, 1), :]
        square = lax.broadcasted_iota(jnp.int32, (rows, rows), 0) == lax.broadcasted_iota(jnp.int32, (rows, rows), 1)
        return jnp.sum(jnp.where(square, row, 0.0), axis=1, keepdims=True)

    def hidden_of(b):
        v = jnp.dot(xall[b], upv[...], preferred_element_type=jnp.float32)
        return (v / (1.0 + jnp.exp(-v))).astype(jnp.bfloat16)

    def keep(s):
        b = block(s, x)
        h = hidden_of(b)
        scale = scale_of(b)
        for q in range(halves):
            acc[s, q] = jnp.dot(h, downv[q], preferred_element_type=jnp.float32) * scale

    def offer(s):
        b = block(s, 1 - x)
        h = hidden_of(b)
        scale = scale_of(b)
        for q in range(halves):
            o = jnp.dot(h, downv[q], preferred_element_type=jnp.float32) * scale
            psend[s, q] = o.astype(jnp.bfloat16)
            if s == column - 1:
                give(s, q)

    def give(s, q):
        copy = remote(psend.at[s, q], xrecv.at[s, q], rx_s.at[s, q], rx_r.at[s, q], pair)
        copy.start()
        sent.append(copy)

    def pass_on(p):
        j, distance, away = place(p)
        slot = jnp.where((distance == 1) & (away < 0), column, j)
        outer = inside(z + away)
        for q in range(halves):
            remote(psend.at[p, q], xrecv.at[p, q], rx_s.at[p, q], rx_r.at[p, q], pair).wait_recv()

            @pl.when(outer)
            def _():
                remote(zsend.at[p, q], zrecv.at[j, q], rz_s.at[p, q], rz_r.at[j, q], pair).wait_recv()
                total = acc[p, q] + xrecv[p, q].astype(jnp.float32) + zrecv[j, q].astype(jnp.float32)
                zsend[p, q] = total.astype(jnp.bfloat16)

            @pl.when(jnp.logical_not(outer))
            def _():
                zsend[p, q] = (acc[p, q] + xrecv[p, q].astype(jnp.float32)).astype(jnp.bfloat16)

            copy = remote(zsend.at[p, q], zrecv.at[slot, q], rz_s.at[p, q], rz_r.at[slot, q], 2 * (z - away) + x)
            copy.start()
            sent.append(copy)

    if column > 1:
        relay(1)
    for copy in local:
        copy.wait()
    for copy in swap:
        copy.wait_recv()
    for s in range(1, n):
        remote(wts.at[core], wall.at[lax.rem(e - s + n, n)], w_s.at[s], w_r.at[s], pair).wait_recv()
    keep(0)
    for p in range(2, column):
        relay(p)
        keep(p - 1)
    for p in range(column):
        if p == column - 1 and p > 0:
            keep(p)
        arrived(p)
        offer(p)
    for p in range(column - 2, -1, -1):
        for q in range(halves):
            give(p, q)
    for p in range(column - 1, 0, -1):
        pass_on(p)
    for q in range(halves):
        remote(psend.at[0, q], xrecv.at[0, q], rx_s.at[0, q], rx_r.at[0, q], pair).wait_recv()
        acc[0, q] += xrecv[0, q].astype(jnp.float32)
        for side, slot in ((1, z), (-1, column)):

            @pl.when(inside(z + side))
            def _():
                remote(zsend.at[0, q], zrecv.at[slot, q], rz_s.at[0, q], rz_r.at[slot, q], pair).wait_recv()
                acc[0, q] += zrecv[slot, q].astype(jnp.float32)

        res[q] = acc[0, q].astype(jnp.bfloat16)
    last = remote(res.at[1 - core], out.at[core], tw_s.at[2], tw_r.at[2])
    last.start()
    mine = pltpu.make_async_copy(res.at[core], out.at[core], loc.at[4])
    mine.start()
    for copy in own_x + own_w + swap + sent:
        copy.wait_send()
    for condition, copy in guarded:
        pl.when(condition)(copy.wait_send)
    mine.wait()
    last.wait_send()
    remote(res.at[1 - core], out.at[1 - core], tw_s.at[2], tw_r.at[2]).wait_recv()


def dense_on_device(tokens, routes, probs, up_weight, down_weight, old_place, new_place):
    source_index = lax.axis_index("expert")
    n = lax.axis_size("expert")
    batches, rows, width = tokens.shape
    hidden_half, half = down_weight.shape[1] // 2, down_weight.shape[2]
    column, chunks = n // 2, 2
    slot_rows = dense_slot_rows(new_place, source_index, n, rows)
    weights = dense_weights(routes, probs, old_place, new_place)
    dma = pltpu.SemaphoreType.DMA
    bf16, f32 = jnp.bfloat16, jnp.float32
    mixed = pl.pallas_call(
        functools.partial(expert_kernel, n, chunks),
        out_shape=jax.ShapeDtypeStruct((batches, rows, half), bf16),
        in_specs=[pl.BlockSpec(memory_space=pl.ANY)] * 4,
        out_specs=pl.BlockSpec(memory_space=pl.ANY),
        scratch_shapes=[
            pltpu.VMEM((n, rows, width), bf16),
            pltpu.VMEM((n, old_place.shape[0], rows), f32),
            pltpu.VMEM((width, 2 * hidden_half), bf16),
            pltpu.VMEM((2, 2 * hidden_half, half), bf16),
            pltpu.VMEM((column, 2, rows, half), f32),
            pltpu.VMEM((column, 2, rows, half), bf16),
            pltpu.VMEM((column, 2, rows, half), bf16),
            pltpu.VMEM((column, 2, rows, half), bf16),
            pltpu.VMEM((column + 1, 2, rows, half), bf16),
            pltpu.VMEM((2, rows, half), bf16),
            dma((5,)), dma((3,)), dma((3,)), dma((n,)), dma((n,)),
            dma((2, chunks)), dma((column, chunks)), dma((column, chunks)), dma((column, chunks)), dma((column, chunks)),
            dma((column, 2)), dma((column, 2)), dma((column, 2)), dma((column + 1, 2)),
        ],
        compiler_params=pltpu.CompilerParams(
            collective_id=0, has_side_effects=True, vmem_limit_bytes=60 * 1024 * 1024
        ),
    )(tokens, weights, up_weight, down_weight)
    return (mixed, slot_rows)


def choose_plan(tokens, routes, probs, up_weight, down_weight, old_place, new_place):
    n = lax.axis_size("expert")
    rows = tokens.shape[1]
    dense = (
        routes.shape[2] == old_place.shape[0] == n
        and n % 2 == 0
        and lax.axis_size("tensor") == tokens.shape[0] == 2
        and up_weight.shape[0] == 1
        and rows % 32 == 0
        and up_weight.shape[2] % 128 == 0
    )
    plan = dense_on_device if dense else on_device
    return plan(tokens, routes, probs, up_weight, down_weight, old_place, new_place)


def solution(mesh):
    placed = (
        P(None, ("groups", "expert"), None),
        P(None, ("groups", "expert"), None),
        P(None, ("groups", "expert"), None),
        P("expert", None, "tensor"),
        P("expert", None, "tensor"),
        P("groups"),
        P("groups"),
    )
    return jax.shard_map(
        choose_plan,
        mesh=mesh,
        in_specs=placed,
        out_specs=(P(None, ("groups", "expert"), "tensor"), P(("groups", "expert"))),
        check_vma=False,
    )
```
